32 devices in a mesh: group: 2 (over y), pre: 4 (over z), head: 2 (over x), sub: 2 (over core).
Axes of the slice: x: 2, y: 2, z: 4, core: 2. Of those that a mesh axis runs over, the one named last changes fastest.
Arguments:
- prefix_query: bfloat16 [8, 256, 2048], P(('group', 'pre'), None, ('head', 'sub')), parts along dimension 0, may hold values from -0.5390625 to 0.5390625
- prefix_key: bfloat16 [8, 256, 2048], P(('group', 'pre'), None, ('head', 'sub')), parts along dimension 0, may hold values from -0.5390625 to 0.5390625
- prefix_value: bfloat16 [8, 256, 2048], P(('group', 'pre'), None, ('head', 'sub')), parts along dimension 0, may hold values from -6 to 6
- prefix_decay: float32 [8, 16, 256], P(('group', 'pre'), ('head', 'sub')), parts along dimension 0, may hold values from -3 to 0
- prefix_beta: float32 [8, 16, 256], P(('group', 'pre'), ('head', 'sub')), parts along dimension 0, may hold values from 0.1 to 0.9
- prefix_cotangent: bfloat16 [8, 256, 2048], P(('group', 'pre'), None, ('head', 'sub')), parts along dimension 0, may hold values from -6 to 6
- branch_query: bfloat16 [32, 128, 2048], P(('group', 'pre'), None, ('head', 'sub')), parts along dimension 0, may hold values from -0.5390625 to 0.5390625
- branch_key: bfloat16 [32, 128, 2048], P(('group', 'pre'), None, ('head', 'sub')), parts along dimension 0, may hold values from -0.5390625 to 0.5390625
- branch_value: bfloat16 [32, 128, 2048], P(('group', 'pre'), None, ('head', 'sub')), parts along dimension 0, may hold values from -6 to 6
- branch_decay: float32 [32, 16, 128], P(('group', 'pre'), ('head', 'sub')), parts along dimension 0, may hold values from -3 to 0
- branch_beta: float32 [32, 16, 128], P(('group', 'pre'), ('head', 'sub')), parts along dimension 0, may hold values from 0.1 to 0.9
- branch_cotangent: bfloat16 [32, 128, 2048], P(('group', 'pre'), None, ('head', 'sub')), parts along dimension 0, may hold values from -6 to 6
- fanout: int32 [8], P('group'), parts along dimension 0, may hold values from 2 to 10, as said below
- placement: int32 [32], P(('group', 'pre')), parts along dimension 0, may hold values from 0 to 15, each once
Outputs:
- branch_out: bfloat16 [32, 128, 2048], P(('group', 'pre'), None, ('head', 'sub')), parts along dimension 0
- trunk_query: bfloat16 [8, 256, 2048], P(('group', 'pre'), None, ('head', 'sub')), parts along dimension 0
- trunk_key: bfloat16 [8, 256, 2048], P(('group', 'pre'), None, ('head', 'sub')), parts along dimension 0
- trunk_value: bfloat16 [8, 256, 2048], P(('group', 'pre'), None, ('head', 'sub')), parts along dimension 0
- trunk_decay: float32 [8, 16, 256], P(('group', 'pre'), ('head', 'sub')), parts along dimension 0
- trunk_beta: float32 [8, 16, 256], P(('group', 'pre'), ('head', 'sub')), parts along dimension 0
- limb_query: bfloat16 [32, 128, 2048], P(('group', 'pre'), None, ('head', 'sub')), parts along dimension 0
- limb_key: bfloat16 [32, 128, 2048], P(('group', 'pre'), None, ('head', 'sub')), parts along dimension 0
- limb_value: bfloat16 [32, 128, 2048], P(('group', 'pre'), None, ('head', 'sub')), parts along dimension 0
- limb_decay: float32 [32, 16, 128], P(('group', 'pre'), ('head', 'sub')), parts along dimension 0
- limb_beta: float32 [32, 16, 128], P(('group', 'pre'), ('head', 'sub')), parts along dimension 0
The draws below stay inside these ranges and needn't reach their ends.
There are 2 independent parts, one for each index of `group`. The reference program is written for one: setup_inputs(seed, part) draws one part's arguments, and reference() takes and returns one part's arrays. A program takes and returns all parts, laid end to end along the dimension named above; each array names one. Nothing has to cross between parts.
Inputs may be any that keep to these rules, and one draw needn't show every extreme that they name: `fanout`: every prefix has at least 2 branches, the counts sum to 16, and some prefix has exactly 10. `placement`: the branches of prefix p have the ranks from bounds_(p-1) (0 for the first) up to bounds_p - 1.
All inputs are finite; a program needn't handle non-finite values.
Results may differ from the reference program's by a relative error of at most 0.015.
Values sent between devices are 32-bit elements; how exact they have to be, the bound alone decides.
A program may use at most 192 MiB of HBM per device.

```python
import jax
import jax.numpy as jnp
from jax import lax

DK = 128
DV = 128
HEADS = 16
SPAN = 128
LP = 256
LB = 128
PREFIXES = 4
BRANCHES = 16
FAN_MAX = 10


def decay_rows(key, count_of_rows, span_length, salt):
    head_key = jax.random.fold_in(key, 11)
    kind_key, slow_key, fast_key = jax.random.split(head_key, 3)
    sequence_length = LP + LB
    slow_share = 0.5
    slow_heads = jax.random.uniform(kind_key, (HEADS,), jnp.float32) < slow_share
    slow_rate = jnp.exp(jax.random.uniform(slow_key, (HEADS,), jnp.float32, jnp.log(0.05 / sequence_length), jnp.log(0.5 / sequence_length)))
    fast_rate = jnp.exp(jax.random.uniform(fast_key, (HEADS,), jnp.float32, jnp.log(0.04), jnp.log(0.07)))
    head_decay_rate = jnp.where(slow_heads, slow_rate, fast_rate)
    private_key = jax.random.fold_in(key, salt)
    row_random_key, token_random_key, flurry_key, level_random_key = jax.random.split(private_key, 4)
    row_scaling = jnp.exp(jax.random.uniform(row_random_key, (count_of_rows, 1, 1), jnp.float32, -0.7, 0.7))
    token_scaling = jax.random.uniform(token_random_key, (count_of_rows, HEADS, span_length), jnp.float32, 0.5, 1.5)
    flurry_list = (jax.random.uniform(flurry_key, (count_of_rows, 1, span_length), jnp.float32) < 2.0 / sequence_length).astype(jnp.float32)
    flurry_depth = jax.random.uniform(level_random_key, (count_of_rows, 1, span_length), jnp.float32, 0.2, 0.5)
    return -head_decay_rate[None, :, None] * row_scaling * token_scaling + flurry_list * jnp.log(1.0 - flurry_depth)


def draw_prefix_decay(key, part):
    return decay_rows(key, PREFIXES, LP, 21)


def draw_branch_decay(key, part):
    return decay_rows(key, BRANCHES, LB, 22)


def draw_fanout(key, part):
    private_key = jax.random.fold_in(key, 3)
    first_key, second_key = jax.random.split(private_key)
    largest = jax.random.randint(first_key, (), 0, PREFIXES)
    counts = jnp.full((PREFIXES,), 2, jnp.int32).at[largest].set(FAN_MAX)
    surplus = BRANCHES - FAN_MAX - 2 * (PREFIXES - 1)

    def add_one(counter, current):
        scores = jax.random.randint(jax.random.fold_in(second_key, counter), (PREFIXES,), 0, 1 << 20) * PREFIXES + jnp.arange(PREFIXES, dtype=jnp.int32)
        has_room = current < FAN_MAX
        chosen = jnp.argmax(jnp.where(has_room, scores, -1))
        return current.at[chosen].add(1)
    return lax.fori_loop(0, surplus, add_one, counts)


def steps_of(own_key, extent, cuts, smallest, top_value):
    def one(dim, blocks):
        draws = jax.random.uniform(jax.random.fold_in(jax.random.fold_in(own_key, 6), dim), (blocks,), jnp.float32, smallest / len(cuts), top_value / len(cuts))
        return jnp.repeat(jnp.exp(draws), extent[dim] // blocks).reshape((-1,) + (1,) * (len(extent) - dim - 1))

    factor_of = one(*cuts[0])
    for cut in cuts[1:]:
        factor_of = factor_of * one(*cut)
    return factor_of


def gaussian(own_key, extent, deviation, most, cuts=(), kind=jnp.bfloat16):
    drawn = jax.random.normal(own_key, extent, jnp.float32) * deviation
    if len(cuts) > 0:
        drawn = steps_of(own_key, extent, cuts, -0.22, 0.18) * drawn
    return jnp.clip(drawn, min=-most, max=most).astype(kind)


def setup_inputs(seed: int = 0, part: int = 0) -> dict:
    keys = jax.random.split(jax.random.key(seed), 15)
    part_keys = jax.random.split(jax.random.fold_in(keys[14], part), 15)
    return {
        "prefix_query": gaussian(part_keys[0], (PREFIXES, LP, HEADS * DK), 0.09, 0.5390625, ((0, 4), (2, 4))),
        "prefix_key": gaussian(part_keys[1], (PREFIXES, LP, HEADS * DK), 0.09, 0.5390625, ((0, 4), (2, 4))),
        "prefix_value": gaussian(part_keys[2], (PREFIXES, LP, HEADS * DV), 1.0, 6.0, ((0, 4), (2, 4))),
        "prefix_decay": draw_prefix_decay(jax.random.fold_in(jax.random.fold_in(keys[14], part), 71), part),
        "prefix_beta": jnp.clip(0.1 + 0.79999997 * jax.random.uniform(part_keys[4], (PREFIXES, HEADS, LP), jnp.float32) ** steps_of(part_keys[4], (PREFIXES, HEADS, LP), ((0, 4), (1, 4)), -0.2, 0.2), 0.1, 0.9),
        "prefix_cotangent": gaussian(part_keys[5], (PREFIXES, LP, HEADS * DV), 1.0, 6.0, ((0, 4), (2, 4))),
        "branch_query": gaussian(part_keys[6], (BRANCHES, LB, HEADS * DK), 0.09, 0.5390625, ((0, 4), (2, 4))),
        "branch_key": gaussian(part_keys[7], (BRANCHES, LB, HEADS * DK), 0.09, 0.5390625, ((0, 4), (2, 4))),
        "branch_value": gaussian(part_keys[8], (BRANCHES, LB, HEADS * DV), 1.0, 6.0, ((0, 4), (2, 4))),
        "branch_decay": draw_branch_decay(jax.random.fold_in(jax.random.fold_in(keys[14], part), 71), part),
        "branch_beta": jnp.clip(0.1 + 0.79999997 * jax.random.uniform(part_keys[10], (BRANCHES, HEADS, LB), jnp.float32) ** steps_of(part_keys[10], (BRANCHES, HEADS, LB), ((0, 4), (1, 4)), -0.2, 0.2), 0.1, 0.9),
        "branch_cotangent": gaussian(part_keys[11], (BRANCHES, LB, HEADS * DV), 1.0, 6.0, ((0, 4), (2, 4))),
        "fanout": draw_fanout(jax.random.fold_in(jax.random.fold_in(keys[14], part), 71), part),
        "placement": jax.random.permutation(part_keys[13], BRANCHES).astype(jnp.int32),
    }


highest_value = lax.Precision.HIGHEST

def unit_rows(matrix):
    return (matrix * lax.rsqrt(lax.optimization_barrier(jnp.sum(matrix * matrix, axis=-1, keepdims=True)) + 1e-06)).astype(jnp.bfloat16)

def block_step(carried_state, inputs):
    query_low, key_low, values, log_decay, beta_rows = inputs
    query_rows = query_low.astype(jnp.float32)
    key_matrix_rows = key_low.astype(jnp.float32)
    block_size = log_decay.shape[-1]
    lower_mask = jnp.tril(jnp.ones((block_size, block_size), jnp.float32))
    identity = jnp.eye(block_size, dtype=jnp.float32)
    strict = lower_mask - identity
    summed_total = jnp.cumsum(log_decay, axis=-1)
    growth_factor = jnp.exp(summed_total)
    log_gaps = summed_total[:, :, None] - summed_total[:, None, :]
    decay_ratio = jnp.exp(jnp.minimum(log_gaps, 0.0)) * lower_mask
    key_gram = jnp.einsum('hck,hdk->hcd', key_matrix_rows, key_matrix_rows, precision=highest_value)
    mixing = strict * beta_rows[:, :, None] * decay_ratio * key_gram
    inverse = identity - mixing
    powered = mixing
    for _ in range(block_size.bit_length() - 2):
        powered = jnp.einsum('hcd,hde->hce', powered, powered, precision=highest_value)
        inverse = jnp.einsum('hcd,hde->hce', inverse, identity + powered, precision=highest_value)
    recalled_values = jnp.einsum('arq,aqz->arz', key_matrix_rows, carried_state, precision=highest_value)
    target = beta_rows[:, :, None] * values - (beta_rows * growth_factor)[:, :, None] * recalled_values
    update_rows = jnp.einsum('hcd,hdv->hcv', inverse, target, precision=highest_value)
    scores = jnp.einsum('hck,hdk->hcd', query_rows, key_matrix_rows, precision=highest_value) * decay_ratio
    output_rows = growth_factor[:, :, None] * jnp.einsum('arq,aqz->arz', query_rows, carried_state, precision=highest_value)
    output_rows = output_rows + jnp.einsum('hcd,hdv->hcv', scores, update_rows, precision=highest_value)
    trailing_decay = jnp.exp(summed_total[:, -1:] - summed_total)
    carried_state = jnp.exp(summed_total[:, -1])[:, None, None] * carried_state + jnp.einsum('ngj,nga->nja', key_matrix_rows * trailing_decay[:, :, None], update_rows, precision=highest_value)
    return (carried_state, output_rows)

def run_rows(start_state, query_rows, key_matrix_rows, values, log_decay, beta_rows):
    count_of_rows, span_length, merged = query_rows.shape
    head_count = log_decay.shape[1]

    def heads_first(matrix):
        return matrix.astype(jnp.float32).reshape(count_of_rows, span_length, head_count, -1).transpose(0, 2, 1, 3)
    blocks = span_length // SPAN

    def split_blocks(matrix):
        shaped = matrix.reshape((count_of_rows * head_count, blocks, SPAN) + matrix.shape[3:])
        return jnp.moveaxis(shaped, 1, 0)
    batched = (split_blocks(unit_rows(heads_first(query_rows))), split_blocks(unit_rows(heads_first(key_matrix_rows))), split_blocks(heads_first(values)), split_blocks(log_decay), split_blocks(beta_rows))
    initial = start_state.reshape((count_of_rows * head_count,) + start_state.shape[2:])
    final, output_rows = lax.scan(block_step, initial, batched)
    output_rows = jnp.moveaxis(output_rows, 0, 1).reshape(count_of_rows, head_count, span_length, -1)
    output_rows = output_rows.transpose(0, 2, 1, 3).reshape(count_of_rows, span_length, -1)
    return (output_rows, final.reshape(start_state.shape))

def reference(prefix_query, prefix_key, prefix_value, prefix_decay, prefix_beta, prefix_cotangent, branch_query, branch_key, branch_value, branch_decay, branch_beta, branch_cotangent, fanout, placement):
    bounds = jnp.cumsum(fanout).astype(jnp.int32)
    parent = lax.optimization_barrier(jnp.sum((bounds[None, :] <= placement[:, None]).astype(jnp.int32), axis=1)).astype(jnp.int32)
    head_count = prefix_decay.shape[1]
    key_size = prefix_query.shape[2] // head_count
    value_size = prefix_value.shape[2] // head_count
    blank_state = jnp.zeros((prefix_query.shape[0], head_count, key_size, value_size), jnp.float32)

    def forward(p_query, p_key, p_value, p_decay, p_beta, b_query, b_key, b_value, b_decay, b_beta):
        prefix_out, prefix_state = run_rows(blank_state, p_query, p_key, p_value, p_decay, p_beta)
        branch_start = jnp.take(prefix_state, parent, axis=0)
        branch_full, unused_state = run_rows(branch_start, b_query, b_key, b_value, b_decay, b_beta)
        return (prefix_out, branch_full)
    (prefix_out, branch_full), pullback = jax.vjp(forward, prefix_query, prefix_key, prefix_value, prefix_decay, prefix_beta, branch_query, branch_key, branch_value, branch_decay, branch_beta)
    gradients = pullback((prefix_cotangent.astype(jnp.float32), branch_cotangent.astype(jnp.float32)))
    return (branch_full.astype(jnp.bfloat16), gradients[0], gradients[1], gradients[2], gradients[3], gradients[4], gradients[5], gradients[6], gradients[7], gradients[8], gradients[9])
```

```python
import functools

import jax
import jax.numpy as jnp
from jax import lax
from jax.experimental import pallas as pl
from jax.experimental.pallas import tpu as pltpu
from jax.sharding import PartitionSpec as P

SPAN = 128
F32 = jnp.float32
BF16 = jnp.bfloat16
HIGH = lax.Precision.HIGHEST
VMEM_BYTES = 40 * 1024 * 1024


def mm(a, b, ca, cb):
    return lax.dot_general(
        a.astype(BF16), b.astype(BF16), (((ca,), (cb,)), ((), ())), preferred_element_type=F32
    )


def nn(a, b):
    return mm(a, b, 1, 0)


def nt(a, b):
    return mm(a, b, 1, 1)


def tn(a, b):
    return mm(a, b, 0, 0)


def exact(a, b, ca, cb):
    return lax.dot_general(
        a, b, (((ca,), (cb,)), ((), ())), precision=HIGH, preferred_element_type=F32
    )


def grid_pair():
    row = lax.broadcasted_iota(jnp.int32, (SPAN, SPAN), 0)
    col = lax.broadcasted_iota(jnp.int32, (SPAN, SPAN), 1)
    return row, col


def rows_total(x):
    return jnp.sum(x, axis=-1, keepdims=True)


def unit(x):
    wide = x.astype(F32)
    scale = lax.rsqrt(rows_total(wide * wide) + 1e-06)
    full = wide * scale
    return scale, full, full.astype(BF16)


def unit_back(scale, full, grad):
    grad = grad.astype(BF16).astype(F32)
    return (scale * (grad - full * rows_total(full * grad))).astype(BF16)


def token_vectors(decay, beta):
    row, col = grid_pair()
    lower = (row >= col).astype(F32)
    sums_col = exact(lower, decay, 1, 1)
    sums_row = exact(decay, lower, 1, 1)
    beta_col = exact((row == col).astype(F32), beta, 1, 1)
    return sums_col, sums_row, beta_col


def ratio_of(g_col, g_row):
    row, col = grid_pair()
    return jnp.where(row >= col, jnp.exp(jnp.minimum(g_col - g_row, 0.0)), 0.0)


def strict_part(x):
    row, col = grid_pair()
    return jnp.where(row > col, x, 0.0)


def inverses(mixings):
    row, col = grid_pair()
    apart = row ^ col
    low = [a.astype(BF16) for a in mixings]
    zero = jnp.zeros((SPAN, SPAN), BF16)
    one = (row == col).astype(BF16)
    inv = [one - jnp.where(apart == 1, a, zero) for a in low]
    size = 2
    while size < SPAN:
        band = (apart >= size) & (apart < 2 * size)
        left = [nn(t, jnp.where(band, a, zero)) for t, a in zip(inv, low)]
        inv = [t - nn(y, t).astype(BF16) for t, y in zip(inv, left)]
        size *= 2
    return inv


def prefix_forward_kernel(heads, blocks, k_ref, v_ref, g_ref, b_ref, state_ref, mid_ref, u_ref, t_ref):
    vecs = [
        token_vectors(g_ref[0, :, pl.ds(n * SPAN, SPAN)], b_ref[0, :, pl.ds(n * SPAN, SPAN)])
        for n in range(blocks)
    ]
    units = [(h, n) for n in range(blocks) for h in range(heads)]
    keys, mixings = {}, []
    for h, n in units:
        sums_col, sums_row, beta_col = vecs[n]
        _, _, key = unit(k_ref[0, pl.ds(n * SPAN, SPAN), pl.ds(h * 128, 128)])
        keys[h, n] = key
        ratio = ratio_of(sums_col[:, h : h + 1], sums_row[h : h + 1, :])
        mixings.append(strict_part(beta_col[:, h : h + 1] * ratio * nt(key, key)))
    inv = dict(zip(units, inverses(mixings)))
    for h, n in units:
        t_ref[n, h] = inv[h, n]
    state = {}
    for n in range(blocks):
        sums_col, sums_row, beta_col = vecs[n]
        for h in range(heads):
            g_col, beta = sums_col[:, h : h + 1], beta_col[:, h : h + 1]
            last = g_col[SPAN - 1 : SPAN, :]
            aim = v_ref[0, pl.ds(n * SPAN, SPAN), pl.ds(h * 128, 128)].astype(F32)
            if n > 0:
                mid_ref[n - 1, h] = state[h]
                aim = aim - jnp.exp(g_col) * nn(keys[h, n], state[h])
            update = nn(inv[h, n], beta * aim)
            u_ref[0, pl.ds(n * SPAN, SPAN), pl.ds(h * 128, 128)] = update.astype(BF16)
            new = tn(keys[h, n].astype(F32) * jnp.exp(last - g_col), update)
            state[h] = new if n == 0 else jnp.exp(last) * state[h] + new
    for h in range(heads):
        state_ref[0, h] = state[h]


def branch_pull_kernel(
    heads, parent_ref, q_ref, k_ref, d_ref, g_ref, b_ref, sums_ref, t_ref, x_ref, dv_ref
):
    j = pl.program_id(0)

    @pl.when(j == 0)
    def _():
        sums_ref[...] = jnp.zeros_like(sums_ref)

    sums_col, sums_row, beta_col = token_vectors(g_ref[0], b_ref[0])
    both, mixings, scores = [], [], []
    for h in range(heads):
        lanes = pl.ds(h * 128, 128)
        _, _, query = unit(q_ref[0, :, lanes])
        _, _, key = unit(k_ref[0, :, lanes])
        pair = jnp.concatenate([query, key], axis=0)
        gram = nt(pair, key)
        ratio = ratio_of(sums_col[:, h : h + 1], sums_row[h : h + 1, :])
        scores.append((gram[:SPAN] * ratio).astype(BF16))
        mixings.append(strict_part(beta_col[:, h : h + 1] * ratio * gram[SPAN:]))
        both.append(pair)
    pulled = [tn(s, d_ref[0, :, pl.ds(h * 128, 128)]) for h, s in enumerate(scores)]
    inv = inverses(mixings)
    target = [tn(t, u) for t, u in zip(inv, pulled)]
    for h in range(heads):
        lanes = pl.ds(h * 128, 128)
        beta = beta_col[:, h : h + 1]
        growth = jnp.exp(sums_col[:, h : h + 1])
        slope = beta * target[h]
        t_ref[0, h] = inv[h]
        x_ref[0, :, lanes] = target[h].astype(BF16)
        dv_ref[0, :, lanes] = slope.astype(BF16)
        cot = d_ref[0, :, lanes].astype(F32)
        right = jnp.concatenate([(growth * cot).astype(BF16), (-growth * slope).astype(BF16)], axis=0)
        sums_ref[parent_ref[j], h] += tn(both[h], right)


def finish(query, key, state, inv_x, beta, g_col, g_row, values, update, cot, dx, next_grad):
    pair = jnp.concatenate([query, key], axis=0)
    gram = nt(pair, key)
    score_gram, key_gram = gram[:SPAN], gram[SPAN:]
    ratio = ratio_of(g_col, g_row)
    growth = jnp.exp(g_col)
    out = None
    aim = values
    if state is not None:
        seen = nn(pair, state)
        aim = values - growth * seen[SPAN:]
    if update is None:
        update = nn(inv_x, beta * aim)
        out = nn(score_gram * ratio, update) + growth * seen[:SPAN]
    grads = jnp.concatenate([cot, dx.astype(BF16)], axis=0)
    outer = nt(grads, update)
    d_score = outer[:SPAN] * ratio
    d_mix = strict_part(outer[SPAN:] * (-beta * ratio))
    stack = jnp.concatenate([d_score.astype(BF16), d_mix.astype(BF16)], axis=0)
    down = nn(stack, key)
    d_query = down[:SPAN]
    d_key = down[SPAN:] + tn(stack, pair)
    mix_part = d_mix * key_gram
    d_ratio = d_score * score_gram + mix_part
    wide_dx = dx.astype(F32)
    d_beta = rows_total(wide_dx * aim + mix_part / beta)
    column = d_ratio
    constant = None
    if state is not None:
        back = nt(grads, state)
        d_query = d_query + growth * back[:SPAN]
        slope = beta * growth
        d_key = d_key - slope * back[SPAN:]
        column = column + growth * (cot.astype(F32) * seen[:SPAN]) - slope * (wide_dx * seen[SPAN:])
    if next_grad is not None:
        last = g_col[SPAN - 1 : SPAN, :]
        trail = jnp.exp(last - g_col) * nt(update, next_grad)
        d_key = d_key + trail
        trailing = trail * key.astype(F32)
        column = column - trailing
        constant = jnp.sum(rows_total(trailing), axis=0, keepdims=True)
        if state is not None:
            product = jnp.sum(rows_total(state * next_grad), axis=0, keepdims=True)
            constant = constant + jnp.exp(last) * product
    return d_query, d_key, d_beta, rows_total(column), jnp.sum(d_ratio, axis=0, keepdims=True), constant, out


def token_rows(columns, rows, betas):
    row, col = grid_pair()
    lower = (row >= col).astype(F32)
    d_decay = exact(jnp.concatenate(columns, axis=1), lower, 0, 0) - exact(
        jnp.concatenate(rows, axis=0), lower, 1, 0
    )
    d_beta = exact(jnp.concatenate(betas, axis=1), (row == col).astype(F32), 0, 0)
    return d_decay, d_beta


def branch_finish_kernel(
    heads, parent_ref, q_ref, k_ref, v_ref, d_ref, g_ref, b_ref, t_ref, x_ref, s_ref,
    o_ref, dq_ref, dk_ref, dg_ref, db_ref,
):
    sums_col, sums_row, beta_col = token_vectors(g_ref[0], b_ref[0])
    columns, rows, betas = [], [], []
    for h in range(heads):
        lanes = pl.ds(h * 128, 128)
        q_scale, q_full, query = unit(q_ref[0, :, lanes])
        k_scale, k_full, key = unit(k_ref[0, :, lanes])
        d_query, d_key, d_beta, column, row, _, out = finish(
            query, key, s_ref[0, h], t_ref[0, h], beta_col[:, h : h + 1],
            sums_col[:, h : h + 1], sums_row[h : h + 1, :], v_ref[0, :, lanes].astype(F32),
            None, d_ref[0, :, lanes], x_ref[0, :, lanes], None,
        )
        o_ref[0, :, lanes] = out.astype(BF16)
        dq_ref[0, :, lanes] = unit_back(q_scale, q_full, d_query)
        dk_ref[0, :, lanes] = unit_back(k_scale, k_full, d_key)
        columns.append(column)
        rows.append(row)
        betas.append(d_beta)
    d_decay, d_beta = token_rows(columns, rows, betas)
    dg_ref[0] = d_decay
    db_ref[0] = d_beta


def prefix_finish_kernel(
    heads, blocks, q_ref, k_ref, v_ref, d_ref, g_ref, b_ref, t_ref, u_ref, mid_ref, sg_ref,
    dq_ref, dk_ref, dv_ref, dg_ref, db_ref,
):
    grads = [sg_ref[0, h] for h in range(heads)]
    for n in reversed(range(blocks)):
        span = pl.ds(n * SPAN, SPAN)
        sums_col, sums_row, beta_col = token_vectors(g_ref[0, :, span], b_ref[0, :, span])
        columns, rows, betas, constants = [], [], [], []
        for h in range(heads):
            lanes = pl.ds(h * 128, 128)
            g_col, g_row = sums_col[:, h : h + 1], sums_row[h : h + 1, :]
            beta = beta_col[:, h : h + 1]
            growth = jnp.exp(g_col)
            last = g_col[SPAN - 1 : SPAN, :]
            q_scale, q_full, query = unit(q_ref[0, span, lanes])
            k_scale, k_full, key = unit(k_ref[0, span, lanes])
            cot = d_ref[0, span, lanes]
            update = u_ref[0, span, lanes]
            state = mid_ref[n - 1, h] if n > 0 else None
            score = nt(query, key) * ratio_of(g_col, g_row)
            d_update = tn(score, cot) + nn(key.astype(F32) * jnp.exp(last - g_col), grads[h])
            dx = tn(t_ref[n, h], d_update)
            slope = beta * dx
            dv_ref[0, span, lanes] = slope.astype(BF16)
            d_query, d_key, d_beta, column, row, constant, _ = finish(
                query, key, state, None, beta, g_col, g_row,
                v_ref[0, span, lanes].astype(F32), update, cot, dx, grads[h],
            )
            if n > 0:
                right = jnp.concatenate(
                    [(growth * cot.astype(F32)).astype(BF16), (-growth * slope).astype(BF16)], axis=0
                )
                pair = jnp.concatenate([query, key], axis=0)
                grads[h] = jnp.exp(last) * grads[h] + tn(pair, right)
            dq_ref[0, span, lanes] = unit_back(q_scale, q_full, d_query)
            dk_ref[0, span, lanes] = unit_back(k_scale, k_full, d_key)
            columns.append(column)
            rows.append(row)
            betas.append(d_beta)
            constants.append(constant)
        d_decay, d_beta = token_rows(columns, rows, betas)
        dg_ref[0, :, span] = d_decay + jnp.concatenate(constants, axis=0)
        db_ref[0, :, span] = d_beta


def whole(shape):
    zeros = (0,) * len(shape)
    return pl.BlockSpec(shape, lambda *_: zeros)


def by_row(shape):
    zeros = (0,) * (len(shape) - 1)
    return pl.BlockSpec((1,) + tuple(shape[1:]), lambda j, *_: (j,) + zeros)


def struct(shape, kind):
    return jax.ShapeDtypeStruct(tuple(shape), kind)


def params():
    return pltpu.CompilerParams(vmem_limit_bytes=VMEM_BYTES)


def cost(flops, moved):
    return pl.CostEstimate(flops=flops, bytes_accessed=moved, transcendentals=0)


def on_device(
    prefix_query,
    prefix_key,
    prefix_value,
    prefix_decay,
    prefix_beta,
    prefix_cotangent,
    branch_query,
    branch_key,
    branch_value,
    branch_decay,
    branch_beta,
    branch_cotangent,
    fanout,
    placement,
):
    heads = prefix_decay.shape[1]
    length = prefix_query.shape[1]
    blocks = length // SPAN
    branches = branch_query.shape[0]
    prefixes = fanout.shape[0]
    upto = jnp.arange(prefixes)[:, None] >= jnp.arange(prefixes)[None, :]
    bounds = jnp.sum(jnp.where(upto, fanout[None, :], 0), axis=1)
    parent = jnp.sum((bounds[None, :] <= placement[:, None]).astype(jnp.int32), axis=1)
    unit_flops = 2 * 128 * 128 * 128

    pq, tq = prefix_query.shape, prefix_decay.shape
    prefix_state, mids, updates, prefix_inv = pl.pallas_call(
        functools.partial(prefix_forward_kernel, heads, blocks),
        out_shape=(
            struct((1, heads, 128, 128), F32),
            struct((max(blocks - 1, 1), heads, 128, 128), F32),
            struct(pq, BF16),
            struct((blocks, heads, SPAN, SPAN), BF16),
        ),
        compiler_params=params(),
        cost_estimate=cost(60 * heads * blocks * unit_flops, 10**6),
        name="prefix_forward",
    )(prefix_key, prefix_value, prefix_decay, prefix_beta)
    all_states = lax.all_gather(prefix_state, "pre", axis=0, tiled=True)

    bq, tb = branch_query.shape, branch_decay.shape
    inv_shape = (branches, heads, SPAN, SPAN)
    sums_shape = (prefixes, heads, 128, 128)
    partial_sums, branch_inv, branch_dx, limb_value = pl.pallas_call(
        functools.partial(branch_pull_kernel, heads),
        grid_spec=pltpu.PrefetchScalarGridSpec(
            num_scalar_prefetch=1,
            grid=(branches,),
            in_specs=[by_row(bq), by_row(bq), by_row(bq), by_row(tb), by_row(tb)],
            out_specs=[whole(sums_shape), by_row(inv_shape), by_row(bq), by_row(bq)],
        ),
        out_shape=(
            struct(sums_shape, F32),
            struct(inv_shape, BF16),
            struct(bq, BF16),
            struct(bq, BF16),
        ),
        compiler_params=params(),
        cost_estimate=cost(80 * heads * branches * unit_flops, 5 * 10**6),
        name="branch_pull",
    )(parent, branch_query, branch_key, branch_cotangent, branch_decay, branch_beta)
    state_grad = lax.psum_scatter(partial_sums, "pre", scatter_dimension=0, tiled=True)

    branch_out, limb_query, limb_key, limb_decay, limb_beta = pl.pallas_call(
        functools.partial(branch_finish_kernel, heads),
        grid_spec=pltpu.PrefetchScalarGridSpec(
            num_scalar_prefetch=1,
            grid=(branches,),
            in_specs=[
                by_row(bq), by_row(bq), by_row(bq), by_row(bq), by_row(tb), by_row(tb),
                by_row(inv_shape), by_row(bq),
                pl.BlockSpec((1, heads, 128, 128), lambda j, parent: (parent[j], 0, 0, 0)),
            ],
            out_specs=[by_row(bq), by_row(bq), by_row(bq), by_row(tb), by_row(tb)],
        ),
        out_shape=(
            struct(bq, BF16), struct(bq, BF16), struct(bq, BF16), struct(tb, F32), struct(tb, F32),
        ),
        compiler_params=params(),
        cost_estimate=cost(80 * heads * branches * unit_flops, 5 * 10**6),
        name="branch_finish",
    )(
        parent, branch_query, branch_key, branch_value, branch_cotangent, branch_decay,
        branch_beta, branch_inv, branch_dx, all_states,
    )

    trunk_query, trunk_key, trunk_value, trunk_decay, trunk_beta = pl.pallas_call(
        functools.partial(prefix_finish_kernel, heads, blocks),
        out_shape=(
            struct(pq, BF16), struct(pq, BF16), struct(pq, BF16), struct(tq, F32), struct(tq, F32),
        ),
        compiler_params=params(),
        cost_estimate=cost(60 * heads * blocks * unit_flops, 2 * 10**6),
        name="prefix_finish",
    )(
        prefix_query, prefix_key, prefix_value, prefix_cotangent, prefix_decay, prefix_beta,
        prefix_inv, updates, mids, state_grad,
    )
    return (
        branch_out,
        trunk_query,
        trunk_key,
        trunk_value,
        trunk_decay,
        trunk_beta,
        limb_query,
        limb_key,
        limb_value,
        limb_decay,
        limb_beta,
    )


def solution(mesh):
    data = P(("group", "pre"), None, ("head", "sub"))
    token = P(("group", "pre"), ("head", "sub"), None)
    in_specs = (
        data, data, data, token, token, data,
        data, data, data, token, token, data,
        P("group"), P(("group", "pre")),
    )
    out_specs = (data, data, data, data, token, token, data, data, data, token, token)
    return jax.shard_map(
        on_device, mesh=mesh, in_specs=in_specs, out_specs=out_specs, check_vma=False
    )
```

```python
import functools

import jax
import jax.numpy as jnp
from jax import lax
from jax.experimental import pallas as pl
from jax.experimental.pallas import tpu as pltpu
from jax.sharding import PartitionSpec as P

SPAN = 128
F32 = jnp.float32
BF16 = jnp.bfloat16
HIGH = lax.Precision.HIGHEST
VMEM_BYTES = 40 * 1024 * 1024


def mm(a, b, ca, cb):
    return lax.dot_general(
        a.astype(BF16), b.astype(BF16), (((ca,), (cb,)), ((), ())), preferred_element_type=F32
    )


def nn(a, b):
    return mm(a, b, 1, 0)


def nt(a, b):
    return mm(a, b, 1, 1)


def tn(a, b):
    return mm(a, b, 0, 0)


def exact(a, b, ca, cb):
    return lax.dot_general(
        a, b, (((ca,), (cb,)), ((), ())), precision=HIGH, preferred_element_type=F32
    )


def grid_pair():
    row = lax.broadcasted_iota(jnp.int32, (SPAN, SPAN), 0)
    col = lax.broadcasted_iota(jnp.int32, (SPAN, SPAN), 1)
    return row, col


def rows_total(x):
    return jnp.sum(x, axis=-1, keepdims=True)


def unit(x):
    wide = x.astype(F32)
    scale = lax.rsqrt(rows_total(wide * wide) + 1e-06)
    full = wide * scale
    return scale, full, full.astype(BF16)


def unit_back(scale, full, grad):
    grad = grad.astype(BF16).astype(F32)
    return (scale * (grad - full * rows_total(full * grad))).astype(BF16)


def token_vectors(decay, beta):
    row, col = grid_pair()
    lower = (row >= col).astype(F32)
    sums_col = exact(lower, decay, 1, 1)
    sums_row = exact(decay, lower, 1, 1)
    beta_col = exact((row == col).astype(F32), beta, 1, 1)
    return sums_col, sums_row, beta_col


def ratio_of(g_col, g_row):
    row, col = grid_pair()
    return jnp.where(row >= col, jnp.exp(jnp.minimum(g_col - g_row, 0.0)), 0.0)


def strict_part(x):
    row, col = grid_pair()
    return jnp.where(row > col, x, 0.0)


def inverses(mixings):
    row, col = grid_pair()
    apart = row ^ col
    low = [a.astype(BF16) for a in mixings]
    zero = jnp.zeros((SPAN, SPAN), BF16)
    one = (row == col).astype(BF16)
    inv = [one - jnp.where(apart == 1, a, zero) for a in low]
    size = 2
    while size < SPAN:
        band = (apart >= size) & (apart < 2 * size)
        left = [nn(t, jnp.where(band, a, zero)) for t, a in zip(inv, low)]
        inv = [t - nn(y, t).astype(BF16) for t, y in zip(inv, left)]
        size *= 2
    return inv


def prefix_forward_kernel(heads, blocks, k_ref, v_ref, g_ref, b_ref, state_ref, mid_ref, u_ref, t_ref):
    vecs = [
        token_vectors(g_ref[0, :, pl.ds(n * SPAN, SPAN)], b_ref[0, :, pl.ds(n * SPAN, SPAN)])
        for n in range(blocks)
    ]
    units = [(h, n) for n in range(blocks) for h in range(heads)]
    keys, mixings = {}, []
    for h, n in units:
        sums_col, sums_row, beta_col = vecs[n]
        _, _, key = unit(k_ref[0, pl.ds(n * SPAN, SPAN), pl.ds(h * 128, 128)])
        keys[h, n] = key
        ratio = ratio_of(sums_col[:, h : h + 1], sums_row[h : h + 1, :])
        mixings.append(strict_part(beta_col[:, h : h + 1] * ratio * nt(key, key)))
    inv = dict(zip(units, inverses(mixings)))
    for h, n in units:
        t_ref[n, h] = inv[h, n]
    state = {}
    for n in range(blocks):
        sums_col, sums_row, beta_col = vecs[n]
        for h in range(heads):
            g_col, beta = sums_col[:, h : h + 1], beta_col[:, h : h + 1]
            last = g_col[SPAN - 1 : SPAN, :]
            aim = v_ref[0, pl.ds(n * SPAN, SPAN), pl.ds(h * 128, 128)].astype(F32)
            if n > 0:
                mid_ref[n - 1, h] = state[h]
                aim = aim - jnp.exp(g_col) * nn(keys[h, n], state[h])
            update = nn(inv[h, n], beta * aim)
            u_ref[0, pl.ds(n * SPAN, SPAN), pl.ds(h * 128, 128)] = update.astype(BF16)
            new = tn(keys[h, n].astype(F32) * jnp.exp(last - g_col), update)
            state[h] = new if n == 0 else jnp.exp(last) * state[h] + new
    for h in range(heads):
        state_ref[0, h] = state[h]


def branch_pull_kernel(
    heads, parent_ref, q_ref, k_ref, d_ref, g_ref, b_ref, sums_ref, t_ref, x_ref, dv_ref
):
    j = pl.program_id(0)

    @pl.when(j == 0)
    def _():
        sums_ref[...] = jnp.zeros_like(sums_ref)

    sums_col, sums_row, beta_col = token_vectors(g_ref[0], b_ref[0])
    both, mixings, scores = [], [], []
    for h in range(heads):
        lanes = pl.ds(h * 128, 128)
        _, _, query = unit(q_ref[0, :, lanes])
        _, _, key = unit(k_ref[0, :, lanes])
        pair = jnp.concatenate([query, key], axis=0)
        gram = nt(pair, key)
        ratio = ratio_of(sums_col[:, h : h + 1], sums_row[h : h + 1, :])
        scores.append((gram[:SPAN] * ratio).astype(BF16))
        mixings.append(strict_part(beta_col[:, h : h + 1] * ratio * gram[SPAN:]))
        both.append(pair)
    pulled = [tn(s, d_ref[0, :, pl.ds(h * 128, 128)]) for h, s in enumerate(scores)]
    inv = inverses(mixings)
    target = [tn(t, u) for t, u in zip(inv, pulled)]
    for h in range(heads):
        lanes = pl.ds(h * 128, 128)
        beta = beta_col[:, h : h + 1]
        growth = jnp.exp(sums_col[:, h : h + 1])
        slope = beta * target[h]
        t_ref[0, h] = inv[h]
        x_ref[0, :, lanes] = target[h].astype(BF16)
        dv_ref[0, :, lanes] = slope.astype(BF16)
        cot = d_ref[0, :, lanes].astype(F32)
        right = jnp.concatenate([(growth * cot).astype(BF16), (-growth * slope).astype(BF16)], axis=0)
        sums_ref[parent_ref[j], h] += tn(both[h], right)


def finish(query, key, state, inv_x, beta, g_col, g_row, values, update, cot, dx, next_grad):
    pair = jnp.concatenate([query, key], axis=0)
    gram = nt(pair, key)
    score_gram, key_gram = gram[:SPAN], gram[SPAN:]
    ratio = ratio_of(g_col, g_row)
    growth = jnp.exp(g_col)
    out = None
    aim = values
    if state is not None:
        seen = nn(pair, state)
        aim = values - growth * seen[SPAN:]
    if update is None:
        update = nn(inv_x, beta * aim)
        out = nn(score_gram * ratio, update) + growth * seen[:SPAN]
    grads = jnp.concatenate([cot, dx.astype(BF16)], axis=0)
    outer = nt(grads, update)
    d_score = outer[:SPAN] * ratio
    d_mix = strict_part(outer[SPAN:] * (-beta * ratio))
    stack = jnp.concatenate([d_score.astype(BF16), d_mix.astype(BF16)], axis=0)
    down = nn(stack, key)
    d_query = down[:SPAN]
    d_key = down[SPAN:] + tn(stack, pair)
    mix_part = d_mix * key_gram
    d_ratio = d_score * score_gram + mix_part
    wide_dx = dx.astype(F32)
    d_beta = rows_total(wide_dx * aim + mix_part / beta)
    column = d_ratio
    constant = None
    if state is not None:
        back = nt(grads, state)
        d_query = d_query + growth * back[:SPAN]
        slope = beta * growth
        d_key = d_key - slope * back[SPAN:]
        column = column + growth * (cot.astype(F32) * seen[:SPAN]) - slope * (wide_dx * seen[SPAN:])
    if next_grad is not None:
        last = g_col[SPAN - 1 : SPAN, :]
        trail = jnp.exp(last - g_col) * nt(update, next_grad)
        d_key = d_key + trail
        trailing = trail * key.astype(F32)
        column = column - trailing
        constant = jnp.sum(rows_total(trailing), axis=0, keepdims=True)
        if state is not None:
            product = jnp.sum(rows_total(state * next_grad), axis=0, keepdims=True)
            constant = constant + jnp.exp(last) * product
    return d_query, d_key, d_beta, rows_total(column), jnp.sum(d_ratio, axis=0, keepdims=True), constant, out


def token_rows(columns, rows, betas):
    row, col = grid_pair()
    lower = (row >= col).astype(F32)
    d_decay = exact(jnp.concatenate(columns, axis=1), lower, 0, 0) - exact(
        jnp.concatenate(rows, axis=0), lower, 1, 0
    )
    d_beta = exact(jnp.concatenate(betas, axis=1), (row == col).astype(F32), 0, 0)
    return d_decay, d_beta


def branch_finish_kernel(
    heads, parent_ref, q_ref, k_ref, v_ref, d_ref, g_ref, b_ref, t_ref, x_ref, s_ref,
    o_ref, dq_ref, dk_ref, dg_ref, db_ref,
):
    sums_col, sums_row, beta_col = token_vectors(g_ref[0], b_ref[0])
    columns, rows, betas = [], [], []
    for h in range(heads):
        lanes = pl.ds(h * 128, 128)
        q_scale, q_full, query = unit(q_ref[0, :, lanes])
        k_scale, k_full, key = unit(k_ref[0, :, lanes])
        d_query, d_key, d_beta, column, row, _, out = finish(
            query, key, s_ref[0, h], t_ref[0, h], beta_col[:, h : h + 1],
            sums_col[:, h : h + 1], sums_row[h : h + 1, :], v_ref[0, :, lanes].astype(F32),
            None, d_ref[0, :, lanes], x_ref[0, :, lanes], None,
        )
        o_ref[0, :, lanes] = out.astype(BF16)
        dq_ref[0, :, lanes] = unit_back(q_scale, q_full, d_query)
        dk_ref[0, :, lanes] = unit_back(k_scale, k_full, d_key)
        columns.append(column)
        rows.append(row)
        betas.append(d_beta)
    d_decay, d_beta = token_rows(columns, rows, betas)
    dg_ref[0] = d_decay
    db_ref[0] = d_beta


def prefix_finish_kernel(
    heads, blocks, q_ref, k_ref, v_ref, d_ref, g_ref, b_ref, t_ref, u_ref, mid_ref, sg_ref,
    dq_ref, dk_ref, dv_ref, dg_ref, db_ref,
):
    grads = [sg_ref[0, h] for h in range(heads)]
    for n in reversed(range(blocks)):
        span = pl.ds(n * SPAN, SPAN)
        sums_col, sums_row, beta_col = token_vectors(g_ref[0, :, span], b_ref[0, :, span])
        columns, rows, betas, constants = [], [], [], []
        for h in range(heads):
            lanes = pl.ds(h * 128, 128)
            g_col, g_row = sums_col[:, h : h + 1], sums_row[h : h + 1, :]
            beta = beta_col[:, h : h + 1]
            growth = jnp.exp(g_col)
            last = g_col[SPAN - 1 : SPAN, :]
            q_scale, q_full, query = unit(q_ref[0, span, lanes])
            k_scale, k_full, key = unit(k_ref[0, span, lanes])
            cot = d_ref[0, span, lanes]
            update = u_ref[0, span, lanes]
            state = mid_ref[n - 1, h] if n > 0 else None
            score = nt(query, key) * ratio_of(g_col, g_row)
            d_update = tn(score, cot) + nn(key.astype(F32) * jnp.exp(last - g_col), grads[h])
            dx = tn(t_ref[n, h], d_update)
            slope = beta * dx
            dv_ref[0, span, lanes] = slope.astype(BF16)
            d_query, d_key, d_beta, column, row, constant, _ = finish(
                query, key, state, None, beta, g_col, g_row,
                v_ref[0, span, lanes].astype(F32), update, cot, dx, grads[h],
            )
            if n > 0:
                right = jnp.concatenate(
                    [(growth * cot.astype(F32)).astype(BF16), (-growth * slope).astype(BF16)], axis=0
                )
                pair = jnp.concatenate([query, key], axis=0)
                grads[h] = jnp.exp(last) * grads[h] + tn(pair, right)
            dq_ref[0, span, lanes] = unit_back(q_scale, q_full, d_query)
            dk_ref[0, span, lanes] = unit_back(k_scale, k_full, d_key)
            columns.append(column)
            rows.append(row)
            betas.append(d_beta)
            constants.append(constant)
        d_decay, d_beta = token_rows(columns, rows, betas)
        dg_ref[0, :, span] = d_decay + jnp.concatenate(constants, axis=0)
        db_ref[0, :, span] = d_beta


def whole(shape):
    zeros = (0,) * len(shape)
    return pl.BlockSpec(shape, lambda *_: zeros)


def by_row(shape):
    zeros = (0,) * (len(shape) - 1)
    return pl.BlockSpec((1,) + tuple(shape[1:]), lambda j, *_: (j,) + zeros)


def struct(shape, kind):
    return jax.ShapeDtypeStruct(tuple(shape), kind)


def params():
    return pltpu.CompilerParams(vmem_limit_bytes=VMEM_BYTES)


def cost(flops, moved):
    return pl.CostEstimate(flops=flops, bytes_accessed=moved, transcendentals=0)


def shifted(x, steps, count):
    return lax.ppermute(x, "pre", [(i, (i + steps) % count) for i in range(count)])


def on_device(
    prefix_query,
    prefix_key,
    prefix_value,
    prefix_decay,
    prefix_beta,
    prefix_cotangent,
    branch_query,
    branch_key,
    branch_value,
    branch_decay,
    branch_beta,
    branch_cotangent,
    fanout,
    placement,
):
    heads = prefix_decay.shape[1]
    length = prefix_query.shape[1]
    blocks = length // SPAN
    branches = branch_query.shape[0]
    prefixes = fanout.shape[0]
    upto = jnp.arange(prefixes)[:, None] >= jnp.arange(prefixes)[None, :]
    bounds = jnp.sum(jnp.where(upto, fanout[None, :], 0), axis=1)
    parent = jnp.sum((bounds[None, :] <= placement[:, None]).astype(jnp.int32), axis=1)
    place = lax.axis_index("pre")
    send_slot = lax.rem(parent - place + prefixes, prefixes)
    state_slot = lax.rem(place - parent + prefixes, prefixes)
    unit_flops = 2 * 128 * 128 * 128

    pq, tq = prefix_query.shape, prefix_decay.shape
    prefix_state, mids, updates, prefix_inv = pl.pallas_call(
        functools.partial(prefix_forward_kernel, heads, blocks),
        out_shape=(
            struct((1, heads, 128, 128), F32),
            struct((max(blocks - 1, 1), heads, 128, 128), F32),
            struct(pq, BF16),
            struct((blocks, heads, SPAN, SPAN), BF16),
        ),
        compiler_params=params(),
        cost_estimate=cost(60 * heads * blocks * unit_flops, 10**6),
        name="prefix_forward",
    )(prefix_key, prefix_value, prefix_decay, prefix_beta)
    all_states = jnp.concatenate(
        [prefix_state] + [shifted(prefix_state, n, prefixes) for n in range(1, prefixes)], axis=0
    )

    bq, tb = branch_query.shape, branch_decay.shape
    inv_shape = (branches, heads, SPAN, SPAN)
    sums_shape = (prefixes, heads, 128, 128)
    partial_sums, branch_inv, branch_dx, limb_value = pl.pallas_call(
        functools.partial(branch_pull_kernel, heads),
        grid_spec=pltpu.PrefetchScalarGridSpec(
            num_scalar_prefetch=1,
            grid=(branches,),
            in_specs=[by_row(bq), by_row(bq), by_row(bq), by_row(tb), by_row(tb)],
            out_specs=[whole(sums_shape), by_row(inv_shape), by_row(bq), by_row(bq)],
        ),
        out_shape=(
            struct(sums_shape, F32),
            struct(inv_shape, BF16),
            struct(bq, BF16),
            struct(bq, BF16),
        ),
        compiler_params=params(),
        cost_estimate=cost(80 * heads * branches * unit_flops, 5 * 10**6),
        name="branch_pull",
    )(send_slot, branch_query, branch_key, branch_cotangent, branch_decay, branch_beta)
    state_grad = partial_sums[:1]
    for n in range(1, prefixes):
        state_grad = state_grad + shifted(partial_sums[n : n + 1], n, prefixes)

    branch_out, limb_query, limb_key, limb_decay, limb_beta = pl.pallas_call(
        functools.partial(branch_finish_kernel, heads),
        grid_spec=pltpu.PrefetchScalarGridSpec(
            num_scalar_prefetch=1,
            grid=(branches,),
            in_specs=[
                by_row(bq), by_row(bq), by_row(bq), by_row(bq), by_row(tb), by_row(tb),
                by_row(inv_shape), by_row(bq),
                pl.BlockSpec((1, heads, 128, 128), lambda j, parent: (parent[j], 0, 0, 0)),
            ],
            out_specs=[by_row(bq), by_row(bq), by_row(bq), by_row(tb), by_row(tb)],
        ),
        out_shape=(
            struct(bq, BF16), struct(bq, BF16), struct(bq, BF16), struct(tb, F32), struct(tb, F32),
        ),
        compiler_params=params(),
        cost_estimate=cost(80 * heads * branches * unit_flops, 5 * 10**6),
        name="branch_finish",
    )(
        state_slot, branch_query, branch_key, branch_value, branch_cotangent, branch_decay,
        branch_beta, branch_inv, branch_dx, all_states,
    )

    trunk_query, trunk_key, trunk_value, trunk_decay, trunk_beta = pl.pallas_call(
        functools.partial(prefix_finish_kernel, heads, blocks),
        out_shape=(
            struct(pq, BF16), struct(pq, BF16), struct(pq, BF16), struct(tq, F32), struct(tq, F32),
        ),
        compiler_params=params(),
        cost_estimate=cost(60 * heads * blocks * unit_flops, 2 * 10**6),
        name="prefix_finish",
    )(
        prefix_query, prefix_key, prefix_value, prefix_cotangent, prefix_decay, prefix_beta,
        prefix_inv, updates, mids, state_grad,
    )
    return (
        branch_out,
        trunk_query,
        trunk_key,
        trunk_value,
        trunk_decay,
        trunk_beta,
        limb_query,
        limb_key,
        limb_value,
        limb_decay,
        limb_beta,
    )


def solution(mesh):
    data = P(("group", "pre"), None, ("head", "sub"))
    token = P(("group", "pre"), ("head", "sub"), None)
    in_specs = (
        data, data, data, token, token, data,
        data, data, data, token, token, data,
        P("group"), P(("group", "pre")),
    )
    out_specs = (data, data, data, data, token, token, data, data, data, token, token)
    return jax.shard_map(
        on_device, mesh=mesh, in_specs=in_specs, out_specs=out_specs, check_vma=False
    )
```
